32 devices in a mesh: pair: 4 (over z), dof: 8 (over y, x, core).
Axes of the slice: x: 2, y: 2, z: 4, core: 2. Of those that a mesh axis runs over, the one named last changes fastest.
Arguments:
- snapshots: float32 [128, 65536], P('pair', 'dof'), may hold values from -600 to 600
Outputs:
- rotated: float32 [128, 65536], P('pair', 'dof')
The draws below stay inside these ranges and needn't reach their ends.
All inputs are finite; a program needn't handle non-finite values.
Results may differ from the reference program's by a relative error of at most 0.0003.
Values sent between devices are 32-bit elements; how exact they have to be, the bound alone decides.
A program may use at most 64 MiB of HBM per device.

```python
import jax
import jax.numpy as jnp
from jax import lax

BLOCK = 16
STEPS = 4
SWEEPS = 2
COLS = 128
DOFS = 65536
N_PAIR = 4


def draw_snapshots(key, part):
    subkeys = jax.random.split(key, 5)
    order_rank = jax.random.permutation(subkeys[0], COLS).astype(jnp.float32)
    jitter = jax.random.uniform(subkeys[1], (COLS,), jnp.float32, 0.0, 0.2)
    column_scale = 0.05 * jnp.exp(5.7 * (order_rank + jitter) / COLS)
    loadings = jnp.clip(jax.random.normal(subkeys[2], (COLS, 3), jnp.float32), -1.5, 1.5)
    noise_part = jnp.clip(jax.random.normal(subkeys[3], (COLS, DOFS), jnp.float32), -5.0, 5.0)
    common_mode = jnp.clip(jax.random.normal(subkeys[4], (3, DOFS), jnp.float32), -1.5, 1.5)
    row_scale = jnp.ones((1, DOFS), jnp.float32)
    shared = loadings[:, 0:1] * common_mode[0:1, :]
    shared = shared + loadings[:, 1:2] * common_mode[1:2, :]
    shared = shared + loadings[:, 2:3] * common_mode[2:3, :]
    values = column_scale[:, None] * row_scale * (noise_part + 1.2 * shared)
    return values.astype(jnp.float32)


def setup_inputs(seed: int = 0) -> dict:
    arg_keys = jax.random.split(jax.random.key(seed), 2)
    snapshots = draw_snapshots(jax.random.fold_in(arg_keys[1], 71), 0)
    return {"snapshots": snapshots}


highest = lax.Precision.HIGHEST

def jacobi(gram_matrix):
    pair_order = gram_matrix.shape[0]
    circle_size = pair_order - 1
    index_row = lax.broadcasted_iota(jnp.int32, (pair_order, pair_order), 0)
    index_col = lax.broadcasted_iota(jnp.int32, (pair_order, pair_order), 1)
    identity_mask = index_row == index_col
    upper_side = index_row < index_col
    indices = jnp.arange(pair_order, dtype=jnp.int32)

    def one_round(round_index, carried):
        gram_now, basis = carried
        shifted = (round_index % circle_size).astype(jnp.int32)
        mirror = (2 * shifted - indices + 2 * circle_size) % circle_size
        partner = jnp.where(indices == circle_size, shifted, jnp.where(indices == shifted, circle_size, mirror)).astype(jnp.int32)
        partner_mask = index_col == partner[:, None]
        zeros = jnp.zeros_like(gram_now)
        upper_part = jnp.where(upper_side, gram_now, gram_now.T)
        coupling = lax.optimization_barrier(jnp.sum(jnp.where(partner_mask, upper_part, zeros), axis=1))
        own_diag = lax.optimization_barrier(jnp.sum(jnp.where(identity_mask, gram_now, zeros), axis=1))
        other_diag = lax.optimization_barrier(jnp.sum(jnp.where(partner_mask, own_diag[None, :] + zeros, zeros), axis=1))
        is_lower = indices < partner
        diag_lower = jnp.where(is_lower, own_diag, other_diag)
        diag_upper = jnp.where(is_lower, other_diag, own_diag)
        spread_diag = diag_upper - diag_lower
        orient = jnp.where(spread_diag >= 0, 1.0, -1.0).astype(gram_now.dtype)
        tangent = orient * 2.0 * coupling / (jnp.abs(spread_diag) + jnp.sqrt(spread_diag * spread_diag + 4.0 * coupling * coupling))
        cosine = 1.0 / jnp.sqrt(1.0 + tangent * tangent)
        sine_part = cosine * tangent
        signed_sine = jnp.where(is_lower, sine_part, -sine_part)
        rotation = jnp.where(identity_mask, cosine[:, None] + zeros, jnp.where(partner_mask, signed_sine[:, None] + zeros, zeros))
        gram_now = jnp.dot(jnp.dot(rotation.T, gram_now, precision=highest), rotation, precision=highest)
        basis = jnp.dot(basis, rotation, precision=highest)
        return (gram_now, basis)
    start = (gram_matrix, jnp.eye(pair_order, dtype=gram_matrix.dtype))
    final_gram, basis = lax.fori_loop(0, SWEEPS * circle_size, one_round, start)
    return basis

def reference(snapshots):
    pair_order = 2 * BLOCK
    pair_rows = snapshots.reshape(N_PAIR, pair_order, DOFS)
    for step_index in range(STEPS):
        gram_matrix = lax.map(lambda pair_block: jnp.dot(pair_block, pair_block.T, precision=highest), pair_rows)
        turned = jax.vmap(jacobi)(gram_matrix)
        moved = lax.map(lambda operands: jnp.dot(operands[0].T, operands[1], precision=highest), (turned, pair_rows))
        top_blocks = moved[:, :BLOCK]
        low_blocks = moved[:, BLOCK:]
        new_top = jnp.concatenate([top_blocks[:1], low_blocks[:1], top_blocks[1:N_PAIR - 1]], axis=0)
        new_low = jnp.concatenate([low_blocks[1:], top_blocks[N_PAIR - 1:]], axis=0)
        pair_rows = jnp.concatenate([new_top, new_low], axis=1)
    return pair_rows.reshape(COLS, DOFS)
```

```python
import functools

import jax
import jax.numpy as jnp
from jax import lax
from jax.experimental import pallas as pl
from jax.experimental.pallas import tpu as pltpu
from jax.sharding import PartitionSpec as P

STEPS = 4
SWEEPS = 2
LANES = 128

highest = lax.Precision.HIGHEST


def dot(a, b, contract):
    return lax.dot_general(
        a, b, ((contract[:1], contract[1:]), ((), ())),
        precision=highest, preferred_element_type=jnp.float32,
    )


def natural_row(place, width, half, order):
    low = place >= width
    local = jnp.where(low, place - width, place)
    problem, k = local // half, local % half
    top_index = jnp.where(k == 0, order - 1, k)
    low_index = jnp.where(k == 0, 0, order - 1 - k)
    return problem * order + jnp.where(low, low_index, top_index), problem


def moved_from(row, half, order, pairs):
    pair, inner = row // order, row % order
    upper = inner < half
    offset = jnp.where(upper, inner, inner - half)
    up_pair = jnp.where(pair <= 1, 0, pair - 1)
    up_half = jnp.where(pair == 1, half, 0)
    last = pair == pairs - 1
    low_pair = jnp.where(last, pair, pair + 1)
    low_half = jnp.where(last, 0, half)
    return jnp.where(upper, up_pair, low_pair) * order + jnp.where(upper, up_half, low_half) + offset


def angles(a, b, c, threshold):
    d = b - a
    c2 = 2.0 * c
    square = d * d + c2 * c2
    big = 2.0 ** 64
    db, cb = d * big, c2 * big
    inverse = jnp.where(
        square < 1e-30, lax.rsqrt(db * db + cb * cb) * big, lax.rsqrt(square)
    )
    co_square = 0.5 + 0.5 * (jnp.abs(d) * inverse)
    root = lax.rsqrt(co_square)
    signed = jnp.where(d >= threshold, c, -c)
    return co_square * root, signed * inverse * root


def kernel(pairs, half, gram_ref, turn_ref):
    order = 2 * half
    circle = order - 1
    rows = pairs * order
    width = -(-pairs * half // LANES) * LANES
    groups = width // LANES
    two = 2 * width
    f32 = jnp.float32

    lane = lax.broadcasted_iota(jnp.int32, (half, LANES), 1)
    row = lax.broadcasted_iota(jnp.int32, (half, LANES), 0)
    k_lane = lane % half
    group_start = lane - k_lane
    diagonal = k_lane == row
    k0, kend = k_lane == 0, k_lane == half - 1
    r0, rend = row == 0, row == half - 1
    row_index = group_start + row
    lane_q = lax.broadcasted_iota(jnp.int32, (order, LANES), 1) % half
    row_q = lax.broadcasted_iota(jnp.int32, (order, LANES), 0)
    q0, qend = lane_q == 0, lane_q == half - 1

    place_c = lax.broadcasted_iota(jnp.int32, (rows, two), 1)
    nat_c, problem_c = natural_row(place_c, width, half, order)
    nat_r = lax.broadcasted_iota(jnp.int32, (rows, two), 0)
    used = problem_c < pairs
    enter = jnp.where(used & (nat_c == nat_r), 1.0, 0.0).astype(f32)
    moved_enter = jnp.where(
        used & (moved_from(nat_c, half, order, pairs) == nat_r), 1.0, 0.0
    ).astype(f32)
    move_row = lax.broadcasted_iota(jnp.int32, (rows, rows), 0)
    move_col = lax.broadcasted_iota(jnp.int32, (rows, rows), 1)
    move = jnp.where(
        moved_from(move_col, half, order, pairs) == move_row, 1.0, 0.0
    ).astype(f32)
    to_next = dot(enter, moved_enter, (0, 0))
    to_end = dot(enter, move, (0, 0))

    def column_shift(top, low, at0, atend):
        left = pltpu.roll(top, LANES - 1, 1)
        right = pltpu.roll(low, 1, 1)
        return (
            jnp.where(at0, top, jnp.where(atend, low, left)),
            jnp.where(at0, left, right),
        )

    def row_shift(top, low):
        up = pltpu.roll(top, half - 1, 0)
        down = pltpu.roll(low, 1, 0)
        return jnp.where(r0, top, jnp.where(rend, low, up)), jnp.where(r0, up, down)

    def one_round(r, states):
        m = r % circle
        t_index, b_index = (m + k_lane) % circle, (m - k_lane + circle) % circle
        swapped = k0 | (t_index > b_index)
        threshold = jnp.where(swapped, jnp.float32(1.2e-38), jnp.float32(0.0))
        out = []
        for aa, bb, ee, dd, qt, qb in states:
            def pick(x):
                s = jnp.sum(jnp.where(diagonal, x, 0.0), axis=0, keepdims=True)
                return jnp.broadcast_to(s, x.shape)

            co_j, si_j = angles(pick(aa), pick(dd), pick(bb), threshold)
            co_i = jnp.take_along_axis(co_j, row_index, axis=1)
            si_i = jnp.take_along_axis(si_j, row_index, axis=1)
            ac, ad = aa * co_j - bb * si_j, aa * si_j + bb * co_j
            ec, ed = ee * co_j - dd * si_j, ee * si_j + dd * co_j
            a1, e1 = co_i * ac - si_i * ec, si_i * ac + co_i * ec
            b1, d1 = co_i * ad - si_i * ed, si_i * ad + co_i * ed
            a2, e2 = row_shift(a1, e1)
            b2, d2 = row_shift(b1, d1)
            a3, b3 = column_shift(a2, b2, k0, kend)
            e3, d3 = column_shift(e2, d2, k0, kend)
            co_q = jnp.concatenate([co_j, co_j], axis=0)
            si_q = jnp.concatenate([si_j, si_j], axis=0)
            q1, q2 = column_shift(
                qt * co_q - qb * si_q, qt * si_q + qb * co_q, q0, qend
            )
            out.append((a3, b3, e3, d3, q1, q2))
        return tuple(out)

    def blocks(gram, g):
        def gather(first_row, first_col):
            total = jnp.zeros((half, LANES), f32)
            for p in range(min(LANES // half, pairs - g * (LANES // half))):
                at = first_row + g * LANES + p * half
                part = gram[at:at + half, first_col + g * LANES:first_col + (g + 1) * LANES]
                total = jnp.where(group_start == p * half, part, total)
            return total

        unused = (group_start // half + g * (LANES // half)) >= pairs
        spare = jnp.where(diagonal, (row + 1).astype(f32), 0.0)
        aa = jnp.where(unused, spare, gather(0, 0))
        bb = jnp.where(unused, 0.0, gather(0, width))
        ee = jnp.where(unused, 0.0, gather(width, 0))
        dd = jnp.where(unused, jnp.where(diagonal, spare + half, 0.0), gather(width, width))
        qt = jnp.where(row_q == lane_q, 1.0, 0.0).astype(f32)
        qb = jnp.where(row_q == lane_q + half, 1.0, 0.0).astype(f32)
        return aa, bb, ee, dd, qt, qb

    def spread(states):
        place_row = lax.broadcasted_iota(jnp.int32, (width, LANES), 0) // half
        place_lane = lax.broadcasted_iota(jnp.int32, (width, LANES), 1) // half
        columns = []
        for which in (4, 5):
            for g in range(groups):
                q = states[g][which]
                mine = place_row == place_lane + g * (LANES // half)
                parts = []
                for h in (0, 1):
                    part = q[h * half:(h + 1) * half]
                    tall = jnp.concatenate([part] * (width // half), axis=0)
                    parts.append(jnp.where(mine, tall, 0.0))
                columns.append(jnp.concatenate(parts, axis=0))
        return jnp.concatenate(columns, axis=1)

    gram = dot(enter, dot(gram_ref[...], enter, (1, 0)), (0, 0))
    total = None
    for step in range(STEPS):
        states = tuple(blocks(gram, g) for g in range(groups))
        states = lax.fori_loop(0, SWEEPS * circle, one_round, states)
        turn = dot(spread(states), to_next if step < STEPS - 1 else to_end, (1, 0))
        total = dot(enter, turn, (1, 0)) if total is None else dot(total, turn, (1, 0))
        if step < STEPS - 1:
            gram = dot(turn, dot(gram, turn, (1, 0)), (0, 0))
    turn_ref[...] = total.T


def body(snapshots):
    order, dofs = snapshots.shape
    pairs = lax.axis_size("pair")
    part = lax.all_to_all(snapshots, "pair", split_axis=1, concat_axis=0, tiled=True)
    gram = lax.psum(jnp.dot(part, part.T, precision=highest), ("pair", "dof"))
    everything = lax.all_gather(snapshots, "pair", axis=0, tiled=True)
    rows = pairs * order
    turn = pl.pallas_call(
        functools.partial(kernel, pairs, order // 2),
        out_shape=jax.ShapeDtypeStruct((rows, rows), jnp.float32),
        in_specs=[pl.BlockSpec(memory_space=pltpu.VMEM)],
        out_specs=pl.BlockSpec(memory_space=pltpu.VMEM),
        compiler_params=pltpu.CompilerParams(vmem_limit_bytes=32 * 2**20),
        cost_estimate=pl.CostEstimate(flops=10**9, bytes_accessed=10**8, transcendentals=0),
        name="rotations",
    )(gram)
    mine = lax.dynamic_slice_in_dim(turn, lax.axis_index("pair") * order, order, 0)
    return jnp.dot(mine, everything, precision=highest)


def solution(mesh):
    in_specs = (P("pair", "dof"),)
    out_specs = P("pair", "dof")
    return jax.shard_map(body, mesh=mesh, in_specs=in_specs, out_specs=out_specs, check_vma=False)
```

```python
import functools

import jax
import jax.numpy as jnp
from jax import lax
from jax.experimental import pallas as pl
from jax.experimental.pallas import tpu as pltpu
from jax.sharding import PartitionSpec as P

STEPS = 4
SWEEPS = 2
LANES = 128

highest = lax.Precision.HIGHEST


def dot(a, b, contract):
    return lax.dot_general(
        a, b, ((contract[:1], contract[1:]), ((), ())),
        precision=highest, preferred_element_type=jnp.float32,
    )


def natural_row(place, width, half, order):
    low = place >= width
    local = jnp.where(low, place - width, place)
    problem, k = local // half, local % half
    top_index = jnp.where(k == 0, order - 1, k)
    low_index = jnp.where(k == 0, 0, order - 1 - k)
    return problem * order + jnp.where(low, low_index, top_index), problem


def moved_from(row, half, order, pairs):
    pair, inner = row // order, row % order
    upper = inner < half
    offset = jnp.where(upper, inner, inner - half)
    up_pair = jnp.where(pair <= 1, 0, pair - 1)
    up_half = jnp.where(pair == 1, half, 0)
    last = pair == pairs - 1
    low_pair = jnp.where(last, pair, pair + 1)
    low_half = jnp.where(last, 0, half)
    return jnp.where(upper, up_pair, low_pair) * order + jnp.where(upper, up_half, low_half) + offset


def angles(a, b, c, threshold):
    d = b - a
    c2 = 2.0 * c
    square = d * d + c2 * c2
    big = 2.0 ** 64
    db, cb = d * big, c2 * big
    inverse = jnp.where(
        square < 1e-30, lax.rsqrt(db * db + cb * cb) * big, lax.rsqrt(square)
    )
    co_square = 0.5 + 0.5 * (jnp.abs(d) * inverse)
    root = lax.rsqrt(co_square)
    signed = jnp.where(d >= threshold, c, -c)
    return co_square * root, signed * inverse * root


def kernel(pairs, half, gram_ref, turn_ref):
    order = 2 * half
    circle = order - 1
    rows = pairs * order
    width = -(-pairs * half // LANES) * LANES
    groups = width // LANES
    two = 2 * width
    f32 = jnp.float32

    lane = lax.broadcasted_iota(jnp.int32, (half, LANES), 1)
    row = lax.broadcasted_iota(jnp.int32, (half, LANES), 0)
    k_lane = lane % half
    group_start = lane - k_lane
    diagonal = k_lane == row
    k0, kend = k_lane == 0, k_lane == half - 1
    r0, rend = row == 0, row == half - 1
    row_index = group_start + row
    lane_q = lax.broadcasted_iota(jnp.int32, (order, LANES), 1) % half
    row_q = lax.broadcasted_iota(jnp.int32, (order, LANES), 0)
    q0, qend = lane_q == 0, lane_q == half - 1

    place_c = lax.broadcasted_iota(jnp.int32, (rows, two), 1)
    nat_c, problem_c = natural_row(place_c, width, half, order)
    nat_r = lax.broadcasted_iota(jnp.int32, (rows, two), 0)
    used = problem_c < pairs
    enter = jnp.where(used & (nat_c == nat_r), 1.0, 0.0).astype(f32)
    moved_enter = jnp.where(
        used & (moved_from(nat_c, half, order, pairs) == nat_r), 1.0, 0.0
    ).astype(f32)
    move_row = lax.broadcasted_iota(jnp.int32, (rows, rows), 0)
    move_col = lax.broadcasted_iota(jnp.int32, (rows, rows), 1)
    move = jnp.where(
        moved_from(move_col, half, order, pairs) == move_row, 1.0, 0.0
    ).astype(f32)
    to_next = dot(enter, moved_enter, (0, 0))
    to_end = dot(enter, move, (0, 0))

    def column_shift(top, low, at0, atend):
        left = pltpu.roll(top, LANES - 1, 1)
        right = pltpu.roll(low, 1, 1)
        return (
            jnp.where(at0, top, jnp.where(atend, low, left)),
            jnp.where(at0, left, right),
        )

    def row_shift(top, low):
        up = pltpu.roll(top, half - 1, 0)
        down = pltpu.roll(low, 1, 0)
        return jnp.where(r0, top, jnp.where(rend, low, up)), jnp.where(r0, up, down)

    def one_round(r, states):
        m = r % circle
        t_index, b_index = (m + k_lane) % circle, (m - k_lane + circle) % circle
        swapped = k0 | (t_index > b_index)
        threshold = jnp.where(swapped, jnp.float32(1.2e-38), jnp.float32(0.0))
        out = []
        for aa, bb, ee, dd, qt, qb in states:
            def pick(x):
                s = jnp.sum(jnp.where(diagonal, x, 0.0), axis=0, keepdims=True)
                return jnp.broadcast_to(s, x.shape)

            co_j, si_j = angles(pick(aa), pick(dd), pick(bb), threshold)
            co_i = jnp.take_along_axis(co_j, row_index, axis=1)
            si_i = jnp.take_along_axis(si_j, row_index, axis=1)
            ac, ad = aa * co_j - bb * si_j, aa * si_j + bb * co_j
            ec, ed = ee * co_j - dd * si_j, ee * si_j + dd * co_j
            a1, e1 = co_i * ac - si_i * ec, si_i * ac + co_i * ec
            b1, d1 = co_i * ad - si_i * ed, si_i * ad + co_i * ed
            a2, e2 = row_shift(a1, e1)
            b2, d2 = row_shift(b1, d1)
            a3, b3 = column_shift(a2, b2, k0, kend)
            e3, d3 = column_shift(e2, d2, k0, kend)
            co_q = jnp.concatenate([co_j, co_j], axis=0)
            si_q = jnp.concatenate([si_j, si_j], axis=0)
            q1, q2 = column_shift(
                qt * co_q - qb * si_q, qt * si_q + qb * co_q, q0, qend
            )
            out.append((a3, b3, e3, d3, q1, q2))
        return tuple(out)

    def blocks(gram, g):
        def gather(first_row, first_col):
            total = jnp.zeros((half, LANES), f32)
            for p in range(min(LANES // half, pairs - g * (LANES // half))):
                at = first_row + g * LANES + p * half
                part = gram[at:at + half, first_col + g * LANES:first_col + (g + 1) * LANES]
                total = jnp.where(group_start == p * half, part, total)
            return total

        unused = (group_start // half + g * (LANES // half)) >= pairs
        spare = jnp.where(diagonal, (row + 1).astype(f32), 0.0)
        aa = jnp.where(unused, spare, gather(0, 0))
        bb = jnp.where(unused, 0.0, gather(0, width))
        ee = jnp.where(unused, 0.0, gather(width, 0))
        dd = jnp.where(unused, jnp.where(diagonal, spare + half, 0.0), gather(width, width))
        qt = jnp.where(row_q == lane_q, 1.0, 0.0).astype(f32)
        qb = jnp.where(row_q == lane_q + half, 1.0, 0.0).astype(f32)
        return aa, bb, ee, dd, qt, qb

    def spread(states):
        place_row = lax.broadcasted_iota(jnp.int32, (width, LANES), 0) // half
        place_lane = lax.broadcasted_iota(jnp.int32, (width, LANES), 1) // half
        columns = []
        for which in (4, 5):
            for g in range(groups):
                q = states[g][which]
                mine = place_row == place_lane + g * (LANES // half)
                parts = []
                for h in (0, 1):
                    part = q[h * half:(h + 1) * half]
                    tall = jnp.concatenate([part] * (width // half), axis=0)
                    parts.append(jnp.where(mine, tall, 0.0))
                columns.append(jnp.concatenate(parts, axis=0))
        return jnp.concatenate(columns, axis=1)

    gram = dot(enter, dot(gram_ref[...], enter, (1, 0)), (0, 0))
    total = None
    for step in range(STEPS):
        states = tuple(blocks(gram, g) for g in range(groups))
        states = lax.fori_loop(0, SWEEPS * circle, one_round, states)
        turn = dot(spread(states), to_next if step < STEPS - 1 else to_end, (1, 0))
        total = dot(enter, turn, (1, 0)) if total is None else dot(total, turn, (1, 0))
        if step < STEPS - 1:
            gram = dot(turn, dot(gram, turn, (1, 0)), (0, 0))
    turn_ref[...] = total.T


def greet(pairs, dofs, pair, dof):
    barrier = pltpu.get_barrier_semaphore()
    for off in range(1, pairs):
        pl.semaphore_signal(
            barrier, inc=1, device_id=(lax.rem(pair + off, pairs), dof),
            device_id_type=pl.DeviceIdType.MESH,
        )
    for off in range(1, dofs):
        pl.semaphore_signal(
            barrier, inc=1, device_id=(pair, lax.rem(dof + off, dofs)),
            device_id_type=pl.DeviceIdType.MESH,
        )
    pl.semaphore_wait(barrier, pairs + dofs - 2)


def send(src, dst, sems, off, device):
    copy = pltpu.make_async_remote_copy(
        src_ref=src, dst_ref=dst, send_sem=sems.at[0, off], recv_sem=sems.at[1, off],
        device_id=device, device_id_type=pl.DeviceIdType.MESH,
    )
    copy.start()
    return copy


def gram_kernel(pairs, dofs, x_ref, part_ref, gram_ref, local, gathered, sums, crossed, whole,
                sem_x, sem_scatter, sem_cross, sem_gather):
    pair, dof = lax.axis_index("pair"), lax.axis_index("dof")
    order = x_ref.shape[0]
    quarter = part_ref.shape[1]
    chunk = sums.shape[0]
    greet(pairs, dofs, pair, dof)

    def rows_of(place):
        return pl.ds(pl.multiple_of(place * order, order), order)

    def columns_of(place):
        return pl.ds(pl.multiple_of(place * quarter, quarter), quarter)

    copies = []
    for off in range(pairs - 1, 0, -1):
        peer = lax.rem(pair + off, pairs)
        copies.append(send(
            x_ref.at[:, columns_of(peer)], part_ref.at[rows_of(pair), :], sem_x, off, (peer, dof)
        ))
    part_ref[rows_of(pair), :] = x_ref[:, columns_of(pair)]
    for copy in copies:
        copy.wait()
    part = part_ref[...]
    local[...] = dot(part, part, (1, 1)).reshape(local.shape)

    copies = []
    for off in range(1, dofs):
        peer = lax.rem(dof + off, dofs)
        copies.append(send(local.at[peer], gathered.at[dof], sem_scatter, off, (pair, peer)))
    gathered[dof] = local[dof]
    for copy in copies:
        copy.wait()
    sums[...] = jnp.sum(gathered[...], axis=0)

    copies = []
    for off in range(1, pairs):
        peer = lax.rem(pair + off, pairs)
        copies.append(send(sums, crossed.at[pair], sem_cross, off, (peer, dof)))
    crossed[pair] = sums[...]
    for copy in copies:
        copy.wait()
    whole[dof] = jnp.sum(crossed[...], axis=0)

    copies = []
    for off in range(1, dofs):
        peer = lax.rem(dof + off, dofs)
        copies.append(send(whole.at[dof], whole.at[dof], sem_gather, off, (pair, peer)))
    for copy in copies:
        copy.wait()
    gram_ref[...] = whole[...].reshape(gram_ref.shape)


def apply_kernel(pairs, turn_ref, part_ref, out_ref, rotated, sem):
    pair, dof = lax.axis_index("pair"), lax.axis_index("dof")
    order = out_ref.shape[0]
    quarter = part_ref.shape[1]
    greet(pairs, 1, pair, dof)

    def turned(place):
        rows = pl.ds(pl.multiple_of(place * order, order), order)
        return dot(turn_ref[rows, :], part_ref[...], (1, 0))

    mine = pl.ds(pl.multiple_of(pair * quarter, quarter), quarter)
    copies = []
    for off in range(pairs - 1, 0, -1):
        peer = lax.rem(pair + off, pairs)
        rotated[off] = turned(peer)
        copies.append(send(rotated.at[off], out_ref.at[:, mine], sem, off, (peer, dof)))
    out_ref[:, mine] = turned(pair)
    for copy in copies:
        copy.wait()


def in_vmem(count):
    return [pl.BlockSpec(memory_space=pltpu.VMEM)] * count


def body(snapshots):
    order, dofs_here = snapshots.shape
    pairs, dofs = lax.axis_size("pair"), lax.axis_size("dof")
    rows, quarter = pairs * order, dofs_here // pairs
    chunk = rows // dofs
    f32 = jnp.float32
    part, gram = pl.pallas_call(
        functools.partial(gram_kernel, pairs, dofs),
        out_shape=(
            jax.ShapeDtypeStruct((rows, quarter), f32),
            jax.ShapeDtypeStruct((rows, rows), f32),
        ),
        in_specs=in_vmem(1),
        out_specs=tuple(in_vmem(2)),
        scratch_shapes=[
            pltpu.VMEM((dofs, chunk, rows), f32),
            pltpu.VMEM((dofs, chunk, rows), f32),
            pltpu.VMEM((chunk, rows), f32),
            pltpu.VMEM((pairs, chunk, rows), f32),
            pltpu.VMEM((dofs, chunk, rows), f32),
            pltpu.SemaphoreType.DMA((2, pairs)),
            pltpu.SemaphoreType.DMA((2, dofs)),
            pltpu.SemaphoreType.DMA((2, pairs)),
            pltpu.SemaphoreType.DMA((2, dofs)),
        ],
        compiler_params=pltpu.CompilerParams(
            vmem_limit_bytes=32 * 2**20, collective_id=0, has_side_effects=True
        ),
        name="gram",
    )(snapshots)
    turn = pl.pallas_call(
        functools.partial(kernel, pairs, order // 2),
        out_shape=jax.ShapeDtypeStruct((rows, rows), f32),
        in_specs=in_vmem(1),
        out_specs=in_vmem(1)[0],
        compiler_params=pltpu.CompilerParams(vmem_limit_bytes=32 * 2**20),
        name="rotations",
    )(gram)
    return pl.pallas_call(
        functools.partial(apply_kernel, pairs),
        out_shape=jax.ShapeDtypeStruct((order, dofs_here), f32),
        in_specs=in_vmem(2),
        out_specs=in_vmem(1)[0],
        scratch_shapes=[
            pltpu.VMEM((pairs, order, quarter), f32),
            pltpu.SemaphoreType.DMA((2, pairs)),
        ],
        compiler_params=pltpu.CompilerParams(
            vmem_limit_bytes=32 * 2**20, collective_id=1, has_side_effects=True
        ),
        name="apply",
    )(turn, part)


def solution(mesh):
    in_specs = (P("pair", "dof"),)
    out_specs = P("pair", "dof")
    return jax.shard_map(body, mesh=mesh, in_specs=in_specs, out_specs=out_specs, check_vma=False)
```

```python
import functools

import jax
import jax.numpy as jnp
from jax import lax
from jax.experimental import pallas as pl
from jax.experimental.pallas import tpu as pltpu
from jax.sharding import PartitionSpec as P

STEPS = 4
SWEEPS = 2
LANES = 128

highest = lax.Precision.HIGHEST


def dot(a, b, contract):
    return lax.dot_general(
        a, b, ((contract[:1], contract[1:]), ((), ())),
        precision=highest, preferred_element_type=jnp.float32,
    )


def natural_row(place, width, half, order):
    low = place >= width
    local = jnp.where(low, place - width, place)
    problem, k = local // half, local % half
    top_index = jnp.where(k == 0, order - 1, k)
    low_index = jnp.where(k == 0, 0, order - 1 - k)
    return problem * order + jnp.where(low, low_index, top_index), problem


def moved_from(row, half, order, pairs):
    pair, inner = row // order, row % order
    upper = inner < half
    offset = jnp.where(upper, inner, inner - half)
    up_pair = jnp.where(pair <= 1, 0, pair - 1)
    up_half = jnp.where(pair == 1, half, 0)
    last = pair == pairs - 1
    low_pair = jnp.where(last, pair, pair + 1)
    low_half = jnp.where(last, 0, half)
    return jnp.where(upper, up_pair, low_pair) * order + jnp.where(upper, up_half, low_half) + offset


def angles(a, b, c, threshold):
    d = b - a
    c2 = 2.0 * c
    square = d * d + c2 * c2
    big = 2.0 ** 64
    db, cb = d * big, c2 * big
    inverse = jnp.where(
        square < 1e-30, lax.rsqrt(db * db + cb * cb) * big, lax.rsqrt(square)
    )
    co_square = 0.5 + 0.5 * (jnp.abs(d) * inverse)
    root = lax.rsqrt(co_square)
    signed = jnp.where(d >= threshold, c, -c)
    return co_square * root, signed * inverse * root


def kernel(pairs, half, gram_ref, turn_ref):
    order = 2 * half
    circle = order - 1
    rows = pairs * order
    width = -(-pairs * half // LANES) * LANES
    groups = width // LANES
    two = 2 * width
    f32 = jnp.float32

    lane = lax.broadcasted_iota(jnp.int32, (half, LANES), 1)
    row = lax.broadcasted_iota(jnp.int32, (half, LANES), 0)
    k_lane = lane % half
    group_start = lane - k_lane
    diagonal = k_lane == row
    k0, kend = k_lane == 0, k_lane == half - 1
    r0, rend = row == 0, row == half - 1
    row_index = group_start + row
    top_from = group_start + jnp.where(r0 | rend, row, row + 1)
    low_from = group_start + jnp.where(r0, 1, row - 1)
    lane_q = lax.broadcasted_iota(jnp.int32, (order, LANES), 1) % half
    row_q = lax.broadcasted_iota(jnp.int32, (order, LANES), 0)
    q0, qend = lane_q == 0, lane_q == half - 1

    place_c = lax.broadcasted_iota(jnp.int32, (rows, two), 1)
    nat_c, problem_c = natural_row(place_c, width, half, order)
    nat_r = lax.broadcasted_iota(jnp.int32, (rows, two), 0)
    used = problem_c < pairs
    enter = jnp.where(used & (nat_c == nat_r), 1.0, 0.0).astype(f32)
    moved_enter = jnp.where(
        used & (moved_from(nat_c, half, order, pairs) == nat_r), 1.0, 0.0
    ).astype(f32)
    move_row = lax.broadcasted_iota(jnp.int32, (rows, rows), 0)
    move_col = lax.broadcasted_iota(jnp.int32, (rows, rows), 1)
    move = jnp.where(
        moved_from(move_col, half, order, pairs) == move_row, 1.0, 0.0
    ).astype(f32)
    to_next = dot(enter, moved_enter, (0, 0))
    to_end = dot(enter, move, (0, 0))

    def column_shift(top, low, at0, atend):
        left = pltpu.roll(top, LANES - 1, 1)
        right = pltpu.roll(low, 1, 1)
        return (
            jnp.where(at0, top, jnp.where(atend, low, left)),
            jnp.where(at0, left, right),
        )

    def row_shift(top, low):
        up = pltpu.roll(top, half - 1, 0)
        down = pltpu.roll(low, 1, 0)
        return jnp.where(r0, top, jnp.where(rend, low, up)), jnp.where(r0, up, down)

    def one_round(r, states):
        m = jnp.where(r >= circle, r - circle, r)
        t_index, b_index = m + row, m - row
        t_index = jnp.where(t_index >= circle, t_index - circle, t_index)
        b_index = jnp.where(b_index < 0, b_index + circle, b_index)
        swapped = r0 | (t_index > b_index)
        threshold = jnp.where(swapped, jnp.float32(1.2e-38), jnp.float32(0.0))
        out = []
        for aa, bb, ee, dd, qt, qb, a_i, d_i, b_i in states:
            def by_lane(x):
                total = jnp.sum(jnp.where(diagonal, x, 0.0), axis=0, keepdims=True)
                return jnp.broadcast_to(total, x.shape)

            co_i, si_i = angles(a_i, d_i, b_i, threshold)
            co_j, si_j = by_lane(co_i), by_lane(si_i)
            a0, e0 = co_i * aa - si_i * ee, si_i * aa + co_i * ee
            b0, d0 = co_i * bb - si_i * dd, si_i * bb + co_i * dd
            a1, b1 = a0 * co_j - b0 * si_j, a0 * si_j + b0 * co_j
            e1, d1 = e0 * co_j - d0 * si_j, e0 * si_j + d0 * co_j
            a2, e2 = row_shift(a1, e1)
            b2, d2 = row_shift(b1, d1)
            a_i = jnp.take_along_axis(jnp.where(rend, b2, a2), top_from, axis=1)
            d_i = jnp.take_along_axis(jnp.where(r0, e2, d2), low_from, axis=1)
            b_i = jnp.take_along_axis(jnp.where(r0, a2, b2), low_from, axis=1)
            a3, b3 = column_shift(a2, b2, k0, kend)
            e3, d3 = column_shift(e2, d2, k0, kend)
            co_q = jnp.concatenate([co_j, co_j], axis=0)
            si_q = jnp.concatenate([si_j, si_j], axis=0)
            q1, q2 = column_shift(
                qt * co_q - qb * si_q, qt * si_q + qb * co_q, q0, qend
            )
            out.append((a3, b3, e3, d3, q1, q2, a_i, d_i, b_i))
        return tuple(out)

    def blocks(gram, g):
        def gather(first_row, first_col):
            total = jnp.zeros((half, LANES), f32)
            for p in range(min(LANES // half, pairs - g * (LANES // half))):
                at = first_row + g * LANES + p * half
                part = gram[at:at + half, first_col + g * LANES:first_col + (g + 1) * LANES]
                total = jnp.where(group_start == p * half, part, total)
            return total

        unused = (group_start // half + g * (LANES // half)) >= pairs
        spare = jnp.where(diagonal, (row + 1).astype(f32), 0.0)
        aa = jnp.where(unused, spare, gather(0, 0))
        bb = jnp.where(unused, 0.0, gather(0, width))
        ee = jnp.where(unused, 0.0, gather(width, 0))
        dd = jnp.where(unused, jnp.where(diagonal, spare + half, 0.0), gather(width, width))
        qt = jnp.where(row_q == lane_q, 1.0, 0.0).astype(f32)
        qb = jnp.where(row_q == lane_q + half, 1.0, 0.0).astype(f32)
        ends = [jnp.take_along_axis(x, row_index, axis=1) for x in (aa, dd, bb)]
        return aa, bb, ee, dd, qt, qb, *ends

    def spread(states):
        place_row = lax.broadcasted_iota(jnp.int32, (width, LANES), 0) // half
        place_lane = lax.broadcasted_iota(jnp.int32, (width, LANES), 1) // half
        columns = []
        for which in (4, 5):
            for g in range(groups):
                q = states[g][which]
                mine = place_row == place_lane + g * (LANES // half)
                parts = []
                for h in (0, 1):
                    part = q[h * half:(h + 1) * half]
                    tall = jnp.concatenate([part] * (width // half), axis=0)
                    parts.append(jnp.where(mine, tall, 0.0))
                columns.append(jnp.concatenate(parts, axis=0))
        return jnp.concatenate(columns, axis=1)

    gram = dot(enter, dot(gram_ref[...], enter, (1, 0)), (0, 0))
    total = None
    for step in range(STEPS):
        states = tuple(blocks(gram, g) for g in range(groups))
        states = lax.fori_loop(0, SWEEPS * circle, one_round, states, unroll=2)
        turn = dot(spread(states), to_next if step < STEPS - 1 else to_end, (1, 0))
        total = dot(enter, turn, (1, 0)) if total is None else dot(total, turn, (1, 0))
        if step < STEPS - 1:
            gram = dot(turn, dot(gram, turn, (1, 0)), (0, 0))
    turn_ref[...] = total.T


def greet(pairs, dofs, pair, dof):
    barrier = pltpu.get_barrier_semaphore()
    for off in range(1, pairs):
        pl.semaphore_signal(
            barrier, inc=1, device_id=(lax.rem(pair + off, pairs), dof),
            device_id_type=pl.DeviceIdType.MESH,
        )
    for off in range(1, dofs):
        pl.semaphore_signal(
            barrier, inc=1, device_id=(pair, lax.rem(dof + off, dofs)),
            device_id_type=pl.DeviceIdType.MESH,
        )
    pl.semaphore_wait(barrier, pairs + dofs - 2)


def send(src, dst, sems, off, device):
    copy = pltpu.make_async_remote_copy(
        src_ref=src, dst_ref=dst, send_sem=sems.at[0, off], recv_sem=sems.at[1, off],
        device_id=device, device_id_type=pl.DeviceIdType.MESH,
    )
    copy.start()
    return copy


def gram_kernel(pairs, dofs, x_ref, part_ref, gram_ref, early, local, gathered, sums, crossed, whole,
                sem_x, sem_scatter, sem_cross, sem_gather):
    pair, dof = lax.axis_index("pair"), lax.axis_index("dof")
    order = x_ref.shape[0]
    quarter = part_ref.shape[1]
    chunk = sums.shape[0]
    greet(pairs, dofs, pair, dof)

    def rows_of(place):
        return pl.ds(pl.multiple_of(place * order, order), order)

    def columns_of(place):
        return pl.ds(pl.multiple_of(place * quarter, quarter), quarter)

    copies = []
    for which, held in ((0, early), (1, part_ref)):
        for off in range(pairs - 1, 0, -1):
            peer = lax.rem(pair + off, pairs)
            copies.append(send(
                x_ref.at[:, columns_of(which * pairs + peer)], held.at[rows_of(pair), :],
                sem_x.at[which], off, (peer, dof),
            ))
        held[rows_of(pair), :] = x_ref[:, columns_of(which * pairs + pair)]
    for copy in copies[:pairs - 1]:
        copy.wait()
    part = early[...]
    gram = dot(part, part, (1, 1))
    for copy in copies[pairs - 1:]:
        copy.wait()
    part = part_ref[...]
    local[...] = (gram + dot(part, part, (1, 1))).reshape(local.shape)

    copies = []
    for off in range(1, dofs):
        peer = lax.rem(dof + off, dofs)
        copies.append(send(local.at[peer], gathered.at[dof], sem_scatter, off, (pair, peer)))
    gathered[dof] = local[dof]
    for copy in copies:
        copy.wait()
    sums[...] = jnp.sum(gathered[...], axis=0)

    copies = []
    for off in range(1, pairs):
        peer = lax.rem(pair + off, pairs)
        copies.append(send(sums, crossed.at[pair], sem_cross, off, (peer, dof)))
    crossed[pair] = sums[...]
    for copy in copies:
        copy.wait()
    whole[dof] = jnp.sum(crossed[...], axis=0)

    copies = []
    for off in range(1, dofs):
        peer = lax.rem(dof + off, dofs)
        copies.append(send(whole.at[dof], whole.at[dof], sem_gather, off, (pair, peer)))
    for copy in copies:
        copy.wait()
    gram_ref[...] = whole[...].reshape(gram_ref.shape)


def apply_kernel(pairs, turn_ref, part_ref, all_ref, out_ref, rotated, sem):
    pair, dof = lax.axis_index("pair"), lax.axis_index("dof")
    order = out_ref.shape[0]
    quarter = part_ref.shape[1]
    greet(pairs, 1, pair, dof)

    def turned(place):
        rows = pl.ds(pl.multiple_of(place * order, order), order)
        return turn_ref[rows, :]

    mine = pl.ds(pl.multiple_of((pairs + pair) * quarter, quarter), quarter)
    copies = []
    for off in range(pairs - 1, 0, -1):
        peer = lax.rem(pair + off, pairs)
        rotated[off] = dot(turned(peer), part_ref[...], (1, 0))
        copies.append(send(rotated.at[off], out_ref.at[:, mine], sem, off, (peer, dof)))
    out_ref[:, mine] = dot(turned(pair), part_ref[...], (1, 0))
    out_ref[:, :pairs * quarter] = dot(turned(pair), all_ref[...], (1, 0))
    for copy in copies:
        copy.wait()


def in_vmem(count):
    return [pl.BlockSpec(memory_space=pltpu.VMEM)] * count


def body(snapshots):
    order, dofs_here = snapshots.shape
    pairs, dofs = lax.axis_size("pair"), lax.axis_size("dof")
    rows, piece = pairs * order, dofs_here // (2 * pairs)
    chunk = rows // dofs
    f32 = jnp.float32
    part, gram = pl.pallas_call(
        functools.partial(gram_kernel, pairs, dofs),
        out_shape=(
            jax.ShapeDtypeStruct((rows, piece), f32),
            jax.ShapeDtypeStruct((rows, rows), f32),
        ),
        in_specs=in_vmem(1),
        out_specs=tuple(in_vmem(2)),
        scratch_shapes=[
            pltpu.VMEM((rows, piece), f32),
            pltpu.VMEM((dofs, chunk, rows), f32),
            pltpu.VMEM((dofs, chunk, rows), f32),
            pltpu.VMEM((chunk, rows), f32),
            pltpu.VMEM((pairs, chunk, rows), f32),
            pltpu.VMEM((dofs, chunk, rows), f32),
            pltpu.SemaphoreType.DMA((2, 2, pairs)),
            pltpu.SemaphoreType.DMA((2, dofs)),
            pltpu.SemaphoreType.DMA((2, pairs)),
            pltpu.SemaphoreType.DMA((2, dofs)),
        ],
        compiler_params=pltpu.CompilerParams(
            vmem_limit_bytes=32 * 2**20, collective_id=0, has_side_effects=True
        ),
        name="gram",
    )(snapshots)
    gram, early = lax.optimization_barrier((gram, snapshots[:, :dofs_here // 2]))
    everything = lax.all_gather(early, "pair", axis=0, tiled=True)
    turn = pl.pallas_call(
        functools.partial(kernel, pairs, order // 2),
        out_shape=jax.ShapeDtypeStruct((rows, rows), f32),
        in_specs=in_vmem(1),
        out_specs=in_vmem(1)[0],
        compiler_params=pltpu.CompilerParams(vmem_limit_bytes=32 * 2**20),
        cost_estimate=pl.CostEstimate(flops=10**9, bytes_accessed=10**8, transcendentals=0),
        name="rotations",
    )(gram)
    return pl.pallas_call(
        functools.partial(apply_kernel, pairs),
        out_shape=jax.ShapeDtypeStruct((order, dofs_here), f32),
        in_specs=in_vmem(3),
        out_specs=in_vmem(1)[0],
        scratch_shapes=[
            pltpu.VMEM((pairs, order, piece), f32),
            pltpu.SemaphoreType.DMA((2, pairs)),
        ],
        compiler_params=pltpu.CompilerParams(
            vmem_limit_bytes=32 * 2**20, collective_id=1, has_side_effects=True
        ),
        name="apply",
    )(turn, part, everything)


def solution(mesh):
    in_specs = (P("pair", "dof"),)
    out_specs = P("pair", "dof")
    return jax.shard_map(body, mesh=mesh, in_specs=in_specs, out_specs=out_specs, check_vma=False)
```

```python
import functools

import jax
import jax.numpy as jnp
from jax import lax
from jax.experimental import pallas as pl
from jax.experimental.pallas import tpu as pltpu
from jax.sharding import PartitionSpec as P

STEPS = 4
SWEEPS = 2
LANES = 128

highest = lax.Precision.HIGHEST


def dot(a, b, contract):
    return lax.dot_general(
        a, b, ((contract[:1], contract[1:]), ((), ())),
        precision=highest, preferred_element_type=jnp.float32,
    )


def natural_row(place, width, half, order):
    low = place >= width
    local = jnp.where(low, place - width, place)
    problem, k = local // half, local % half
    top_index = jnp.where(k == 0, order - 1, k)
    low_index = jnp.where(k == 0, 0, order - 1 - k)
    return problem * order + jnp.where(low, low_index, top_index), problem


def moved_from(row, half, order, pairs):
    pair, inner = row // order, row % order
    upper = inner < half
    offset = jnp.where(upper, inner, inner - half)
    up_pair = jnp.where(pair <= 1, 0, pair - 1)
    up_half = jnp.where(pair == 1, half, 0)
    last = pair == pairs - 1
    low_pair = jnp.where(last, pair, pair + 1)
    low_half = jnp.where(last, 0, half)
    return jnp.where(upper, up_pair, low_pair) * order + jnp.where(upper, up_half, low_half) + offset


def angles(a, b, c, threshold):
    d = b - a
    c2 = 2.0 * c
    square = d * d + c2 * c2
    big = 2.0 ** 64
    db, cb = d * big, c2 * big
    inverse = jnp.where(
        square < 1e-30, lax.rsqrt(db * db + cb * cb) * big, lax.rsqrt(square)
    )
    co_square = 0.5 + 0.5 * (jnp.abs(d) * inverse)
    root = lax.rsqrt(co_square)
    signed = jnp.where(d >= threshold, c, -c)
    return co_square * root, signed * inverse * root


def kernel(pairs, half, gram_ref, turn_ref):
    order = 2 * half
    circle = order - 1
    rows = pairs * order
    width = -(-pairs * half // LANES) * LANES
    groups = width // LANES
    two = 2 * width
    f32 = jnp.float32

    lane = lax.broadcasted_iota(jnp.int32, (half, LANES), 1)
    row = lax.broadcasted_iota(jnp.int32, (half, LANES), 0)
    k_lane = lane % half
    group_start = lane - k_lane
    diagonal = k_lane == row
    k0, kend = k_lane == 0, k_lane == half - 1
    r0, rend = row == 0, row == half - 1
    row_index = group_start + row
    top_from = group_start + jnp.where(r0 | rend, row, row + 1)
    low_from = group_start + jnp.where(r0, 1, row - 1)
    lane_q = lax.broadcasted_iota(jnp.int32, (order, LANES), 1) % half
    row_q = lax.broadcasted_iota(jnp.int32, (order, LANES), 0)
    q0, qend = lane_q == 0, lane_q == half - 1

    place_c = lax.broadcasted_iota(jnp.int32, (rows, two), 1)
    nat_c, problem_c = natural_row(place_c, width, half, order)
    nat_r = lax.broadcasted_iota(jnp.int32, (rows, two), 0)
    used = problem_c < pairs
    enter = jnp.where(used & (nat_c == nat_r), 1.0, 0.0).astype(f32)
    moved_enter = jnp.where(
        used & (moved_from(nat_c, half, order, pairs) == nat_r), 1.0, 0.0
    ).astype(f32)
    move_row = lax.broadcasted_iota(jnp.int32, (rows, rows), 0)
    move_col = lax.broadcasted_iota(jnp.int32, (rows, rows), 1)
    move = jnp.where(
        moved_from(move_col, half, order, pairs) == move_row, 1.0, 0.0
    ).astype(f32)
    to_next = dot(enter, moved_enter, (0, 0))
    to_end = dot(enter, move, (0, 0))

    def column_shift(top, low, at0, atend):
        left = pltpu.roll(top, LANES - 1, 1)
        right = pltpu.roll(low, 1, 1)
        return (
            jnp.where(at0, top, jnp.where(atend, low, left)),
            jnp.where(at0, left, right),
        )

    def row_shift(top, low):
        up = pltpu.roll(top, half - 1, 0)
        down = pltpu.roll(low, 1, 0)
        return jnp.where(r0, top, jnp.where(rend, low, up)), jnp.where(r0, up, down)

    def one_round(r, states):
        m = jnp.where(r >= circle, r - circle, r)
        t_index, b_index = m + row, m - row
        t_index = jnp.where(t_index >= circle, t_index - circle, t_index)
        b_index = jnp.where(b_index < 0, b_index + circle, b_index)
        swapped = r0 | (t_index > b_index)
        threshold = jnp.where(swapped, jnp.float32(1.2e-38), jnp.float32(0.0))
        out = []
        for aa, bb, ee, dd, qt, qb, a_i, d_i, b_i in states:
            def by_lane(x):
                total = jnp.sum(jnp.where(diagonal, x, 0.0), axis=0, keepdims=True)
                return jnp.broadcast_to(total, x.shape)

            co_i, si_i = angles(a_i, d_i, b_i, threshold)
            co_j, si_j = by_lane(co_i), by_lane(si_i)
            a0, e0 = co_i * aa - si_i * ee, si_i * aa + co_i * ee
            b0, d0 = co_i * bb - si_i * dd, si_i * bb + co_i * dd
            a1, b1 = a0 * co_j - b0 * si_j, a0 * si_j + b0 * co_j
            e1, d1 = e0 * co_j - d0 * si_j, e0 * si_j + d0 * co_j
            a2, e2 = row_shift(a1, e1)
            b2, d2 = row_shift(b1, d1)
            a_i = jnp.take_along_axis(jnp.where(rend, b2, a2), top_from, axis=1)
            d_i = jnp.take_along_axis(jnp.where(r0, e2, d2), low_from, axis=1)
            b_i = jnp.take_along_axis(jnp.where(r0, a2, b2), low_from, axis=1)
            a3, b3 = column_shift(a2, b2, k0, kend)
            e3, d3 = column_shift(e2, d2, k0, kend)
            co_q = jnp.concatenate([co_j, co_j], axis=0)
            si_q = jnp.concatenate([si_j, si_j], axis=0)
            q1, q2 = column_shift(
                qt * co_q - qb * si_q, qt * si_q + qb * co_q, q0, qend
            )
            out.append((a3, b3, e3, d3, q1, q2, a_i, d_i, b_i))
        return tuple(out)

    def blocks(gram, g):
        def gather(first_row, first_col):
            total = jnp.zeros((half, LANES), f32)
            for p in range(min(LANES // half, pairs - g * (LANES // half))):
                at = first_row + g * LANES + p * half
                part = gram[at:at + half, first_col + g * LANES:first_col + (g + 1) * LANES]
                total = jnp.where(group_start == p * half, part, total)
            return total

        unused = (group_start // half + g * (LANES // half)) >= pairs
        spare = jnp.where(diagonal, (row + 1).astype(f32), 0.0)
        aa = jnp.where(unused, spare, gather(0, 0))
        bb = jnp.where(unused, 0.0, gather(0, width))
        ee = jnp.where(unused, 0.0, gather(width, 0))
        dd = jnp.where(unused, jnp.where(diagonal, spare + half, 0.0), gather(width, width))
        qt = jnp.where(row_q == lane_q, 1.0, 0.0).astype(f32)
        qb = jnp.where(row_q == lane_q + half, 1.0, 0.0).astype(f32)
        ends = [jnp.take_along_axis(x, row_index, axis=1) for x in (aa, dd, bb)]
        return aa, bb, ee, dd, qt, qb, *ends

    def spread(states):
        place_row = lax.broadcasted_iota(jnp.int32, (width, LANES), 0) // half
        place_lane = lax.broadcasted_iota(jnp.int32, (width, LANES), 1) // half
        columns = []
        for which in (4, 5):
            for g in range(groups):
                q = states[g][which]
                mine = place_row == place_lane + g * (LANES // half)
                parts = []
                for h in (0, 1):
                    part = q[h * half:(h + 1) * half]
                    tall = jnp.concatenate([part] * (width // half), axis=0)
                    parts.append(jnp.where(mine, tall, 0.0))
                columns.append(jnp.concatenate(parts, axis=0))
        return jnp.concatenate(columns, axis=1)

    gram = dot(enter, dot(gram_ref[...], enter, (1, 0)), (0, 0))
    total = None
    for step in range(STEPS):
        states = tuple(blocks(gram, g) for g in range(groups))
        states = lax.fori_loop(0, SWEEPS * circle, one_round, states, unroll=2)
        turn = dot(spread(states), to_next if step < STEPS - 1 else to_end, (1, 0))
        total = dot(enter, turn, (1, 0)) if total is None else dot(total, turn, (1, 0))
        if step < STEPS - 1:
            gram = dot(turn, dot(gram, turn, (1, 0)), (0, 0))
    turn_ref[...] = total.T


def greet(pairs, dofs, pair, dof):
    barrier = pltpu.get_barrier_semaphore()
    for off in range(1, pairs):
        pl.semaphore_signal(
            barrier, inc=1, device_id=(lax.rem(pair + off, pairs), dof),
            device_id_type=pl.DeviceIdType.MESH,
        )
    for off in range(1, dofs):
        pl.semaphore_signal(
            barrier, inc=1, device_id=(pair, lax.rem(dof + off, dofs)),
            device_id_type=pl.DeviceIdType.MESH,
        )
    pl.semaphore_wait(barrier, pairs + dofs - 2)


def send(src, dst, sems, off, device):
    copy = pltpu.make_async_remote_copy(
        src_ref=src, dst_ref=dst, send_sem=sems.at[0, off], recv_sem=sems.at[1, off],
        device_id=device, device_id_type=pl.DeviceIdType.MESH,
    )
    copy.start()
    return copy


def gram_kernel(pairs, dofs, x_ref, part_ref, gram_ref, first_ref, early, local, gathered, sums, crossed, whole,
                sem_x, sem_scatter, sem_cross, sem_gather):
    pair, dof = lax.axis_index("pair"), lax.axis_index("dof")
    order = x_ref.shape[0]
    early_width, late_width = early.shape[1], part_ref.shape[1]
    greet(pairs, dofs, pair, dof)

    def rows_of(place):
        return pl.ds(pl.multiple_of(place * order, order), order)

    def early_columns(place):
        return pl.ds(pl.multiple_of(place * early_width, LANES), early_width)

    def late_columns(place):
        at = pairs * early_width + place * late_width
        return pl.ds(pl.multiple_of(at, LANES), late_width)

    copies = []
    for which, held, columns in ((0, early, early_columns), (1, part_ref, late_columns)):
        for off in range(pairs - 1, 0, -1):
            peer = lax.rem(pair + off, pairs)
            copies.append(send(
                x_ref.at[:, columns(peer)], held.at[rows_of(pair), :],
                sem_x.at[which], off, (peer, dof),
            ))
        held[rows_of(pair), :] = x_ref[:, columns(pair)]
    first_ref[...] = x_ref[:, :pairs * early_width]
    for copy in copies[:pairs - 1]:
        copy.wait()
    part = early[...]
    gram = dot(part, part, (1, 1))
    for copy in copies[pairs - 1:]:
        copy.wait()
    part = part_ref[...]
    local[...] = (gram + dot(part, part, (1, 1))).reshape(local.shape)

    copies = []
    for off in range(1, dofs):
        peer = lax.rem(dof + off, dofs)
        copies.append(send(local.at[peer], gathered.at[dof], sem_scatter, off, (pair, peer)))
    gathered[dof] = local[dof]
    for copy in copies:
        copy.wait()
    sums[...] = jnp.sum(gathered[...], axis=0)

    copies = []
    for off in range(1, pairs):
        peer = lax.rem(pair + off, pairs)
        copies.append(send(sums, crossed.at[pair], sem_cross, off, (peer, dof)))
    crossed[pair] = sums[...]
    for copy in copies:
        copy.wait()
    whole[dof] = jnp.sum(crossed[...], axis=0)

    copies = []
    for off in range(1, dofs):
        peer = lax.rem(dof + off, dofs)
        copies.append(send(whole.at[dof], whole.at[dof], sem_gather, off, (pair, peer)))
    for copy in copies:
        copy.wait()
    gram_ref[...] = whole[...].reshape(gram_ref.shape)


def apply_kernel(pairs, turn_ref, part_ref, *refs):
    *shifted, out_ref, rotated, everything, sem = refs
    pair, dof = lax.axis_index("pair"), lax.axis_index("dof")
    order = out_ref.shape[0]
    quarter = part_ref.shape[1]
    greet(pairs, 1, pair, dof)

    def turned(place):
        rows = pl.ds(pl.multiple_of(place * order, order), order)
        return turn_ref[rows, :]

    early_all = everything.shape[1]
    mine = pl.ds(pl.multiple_of(early_all + pair * quarter, LANES), quarter)
    copies = []
    for off in range(pairs - 1, 0, -1):
        peer = lax.rem(pair + off, pairs)
        rotated[off] = dot(turned(peer), part_ref[...], (1, 0))
        copies.append(send(rotated.at[off], out_ref.at[:, mine], sem, off, (peer, dof)))
    out_ref[:, mine] = dot(turned(pair), part_ref[...], (1, 0))
    for off, block in enumerate(shifted):
        source = lax.rem(pair + pairs - off, pairs)
        everything[pl.ds(pl.multiple_of(source * order, order), order), :] = block[...]
    out_ref[:, :early_all] = dot(turned(pair), everything[...], (1, 0))
    for copy in copies:
        copy.wait()


def in_vmem(count):
    return [pl.BlockSpec(memory_space=pltpu.VMEM)] * count


def body(snapshots):
    order, dofs_here = snapshots.shape
    pairs, dofs = lax.axis_size("pair"), lax.axis_size("dof")
    rows, share = pairs * order, dofs_here // pairs
    early = max(share * 6 // 16 // LANES, 1) * LANES
    late = share - early
    chunk = rows // dofs
    f32 = jnp.float32
    part, gram, first = pl.pallas_call(
        functools.partial(gram_kernel, pairs, dofs),
        out_shape=(
            jax.ShapeDtypeStruct((rows, late), f32),
            jax.ShapeDtypeStruct((rows, rows), f32),
            jax.ShapeDtypeStruct((order, pairs * early), f32),
        ),
        in_specs=in_vmem(1),
        out_specs=tuple(in_vmem(3)),
        scratch_shapes=[
            pltpu.VMEM((rows, early), f32),
            pltpu.VMEM((dofs, chunk, rows), f32),
            pltpu.VMEM((dofs, chunk, rows), f32),
            pltpu.VMEM((chunk, rows), f32),
            pltpu.VMEM((pairs, chunk, rows), f32),
            pltpu.VMEM((dofs, chunk, rows), f32),
            pltpu.SemaphoreType.DMA((2, 2, pairs)),
            pltpu.SemaphoreType.DMA((2, dofs)),
            pltpu.SemaphoreType.DMA((2, pairs)),
            pltpu.SemaphoreType.DMA((2, dofs)),
        ],
        compiler_params=pltpu.CompilerParams(
            vmem_limit_bytes=32 * 2**20, collective_id=0, has_side_effects=True
        ),
        name="gram",
    )(snapshots)
    shifted = [first] + [
        lax.ppermute(first, "pair", [(i, (i + off) % pairs) for i in range(pairs)])
        for off in range(1, pairs)
    ]
    turn = pl.pallas_call(
        functools.partial(kernel, pairs, order // 2),
        out_shape=jax.ShapeDtypeStruct((rows, rows), f32),
        in_specs=in_vmem(1),
        out_specs=in_vmem(1)[0],
        compiler_params=pltpu.CompilerParams(vmem_limit_bytes=32 * 2**20),
        cost_estimate=pl.CostEstimate(flops=10**9, bytes_accessed=10**8, transcendentals=0),
        name="rotations",
    )(gram)
    return pl.pallas_call(
        functools.partial(apply_kernel, pairs),
        out_shape=jax.ShapeDtypeStruct((order, dofs_here), f32),
        in_specs=in_vmem(2 + pairs),
        out_specs=in_vmem(1)[0],
        scratch_shapes=[
            pltpu.VMEM((pairs, order, late), f32),
            pltpu.VMEM((rows, pairs * early), f32),
            pltpu.SemaphoreType.DMA((2, pairs)),
        ],
        compiler_params=pltpu.CompilerParams(
            vmem_limit_bytes=32 * 2**20, collective_id=1, has_side_effects=True
        ),
        name="apply",
    )(turn, part, *shifted)


def solution(mesh):
    in_specs = (P("pair", "dof"),)
    out_specs = P("pair", "dof")
    return jax.shard_map(body, mesh=mesh, in_specs=in_specs, out_specs=out_specs, check_vma=False)
```
